512 devices in a mesh: pipe: 16 (over x_hi, z), tensor: 8 (over y), dp: 4 (over x_lo, core).
Axes of the slice: x: 4 (x_hi: 2, x_lo: 2; x = x_hi * 2 + x_lo), y: 8, z: 8, core: 2. Of those that a mesh axis runs over, the one named last changes fastest.
Arguments:
- sent_act: bfloat16 [4, 16, 256, 12288], P('dp', 'pipe', None, 'tensor'), may hold values from -64 to 64
- sent_grad: bfloat16 [4, 16, 256, 12288], P('dp', 'pipe', None, 'tensor'), may hold values from -64 to 64
- evicted: bfloat16 [4, 16, 256, 12288], P('dp', 'pipe', None, 'tensor'), may hold values from -64 to 64
- layer_params: float32 [16, 3, 12288], P('pipe', None, 'tensor'), may hold values from -8 to 8
- doc_ids: int32 [4, 16, 2, 256], P('dp', 'pipe'), may hold values from 0 to 3, never falling along the last dimension, each value on 1 to 128 neighbouring positions
Outputs:
- new_act: bfloat16 [4, 16, 256, 12288], P('dp', 'pipe', None, 'tensor')
- new_grad: bfloat16 [4, 16, 256, 12288], P('dp', 'pipe', None, 'tensor')
- kept_input: bfloat16 [4, 16, 256, 12288], P('dp', 'pipe', None, 'tensor')
- param_grad: float32 [16, 3, 12288], P('pipe', None, 'tensor')
The draws below stay inside these ranges and needn't reach their ends.
All inputs are finite; a program needn't handle non-finite values.
Results may differ from the reference program's by a relative error of at most 0.0025.
The reference program's roundings to bfloat16 on the way (of `query`, `probs16` and `grad_scores`) count: a program that leaves them out, or rounds other values in their place, can miss the bound.
Values may be sent and summed in bfloat16 or wider, within the bound.
No kernel may reach another device: no remote copies, remote signals or barrier semaphores. Data moves between devices by JAX's collectives and lax.ppermute only.
A program may use at most 64 MiB of HBM per device.

```python
import math
import jax
import jax.numpy as jnp
import numpy as np
from jax import lax

D = 12288
HEAD = 128
TOK = 256
SEGS = 4
N_PIPE = 16
N_DP = 4


def shape_field(key, noise, row_top):
    key_row, key_col, key_block, key_offset, key_sign = jax.random.split(key, 5)
    block_index = (jnp.arange(D) * 8 // D).astype(jnp.int32)
    block_scale = jnp.exp(jax.random.uniform(key_block, (8,), jnp.float32, math.log(0.5), math.log(2.0)))
    col_scale = jnp.take(block_scale, block_index) * jax.random.uniform(key_col, (D,), jnp.float32, 0.5, 1.5)
    row_shape = (N_DP, N_PIPE, TOK, 1)
    row_scale = jnp.exp(jax.random.uniform(key_row, row_shape, jnp.float32, 0.0, math.log(row_top)))
    offset_size = jax.random.uniform(key_offset, row_shape, jnp.float32, 1.0, 2.5)
    offset_sign = jnp.where(jax.random.bernoulli(key_sign, 0.5, row_shape), 1.0, -1.0)
    return jnp.clip(0.5 * row_scale * (noise * col_scale + offset_size * offset_sign), -64.0, 64.0)


def field_noise(key):
    key_main = jax.random.fold_in(key, 0)
    shape = (N_DP, N_PIPE, TOK, D)
    main = jax.random.normal(key_main, shape, jnp.float32)
    return main


def draw_sent_act(key, part):
    key = jax.random.fold_in(key, 11)
    key_noise, key_shape = jax.random.split(key, 2)
    return shape_field(key_shape, field_noise(key_noise), 3.0).astype(jnp.bfloat16)


def draw_sent_grad(key, part):
    key = jax.random.fold_in(key, 12)
    key_noise, key_shape = jax.random.split(key, 2)
    return shape_field(key_shape, field_noise(key_noise), 3.0).astype(jnp.bfloat16)


def draw_evicted(key, part):
    key = jax.random.fold_in(key, 13)
    key_noise, key_shape = jax.random.split(key, 2)
    return shape_field(key_shape, field_noise(key_noise), 3.0).astype(jnp.bfloat16)


def draw_layer_params(key, part):
    key = jax.random.fold_in(key, 23)
    key_gain, key_query, key_keys, key_factor = jax.random.split(key, 4)
    gain = jax.random.uniform(key_gain, (N_PIPE, 1, D), jnp.float32, 0.6, 1.6)
    factor = jnp.exp(jax.random.uniform(key_factor, (N_PIPE, 2, D), jnp.float32, math.log(0.5), math.log(2.0)))
    base = jnp.stack([jax.random.normal(key_query, (N_PIPE, D), jnp.float32), jax.random.normal(key_keys, (N_PIPE, D), jnp.float32)], 1)
    scales = base * factor
    return jnp.clip(jnp.concatenate([gain, scales], 1), -8.0, 8.0)


def length_profile(number_of, total, reach, skew):
    portions = [(1 << 20) // math.isqrt(rank ** skew) + 1 for rank in range(2, number_of + 1)]
    surplus, holding = total - reach - (number_of - 1), [1] * (number_of - 1)
    while surplus > 0:
        free = [i for i in range(number_of - 1) if holding[i] < reach]
        mass, left = sum([portions[i] for i in free]), surplus
        for i in free:
            extra = min(reach - holding[i], max(1, left * portions[i] // mass), surplus)
            holding[i] = holding[i] + extra
            surplus = surplus - extra
    return np.array([reach] + holding)


def uneven_parts(rng, amount, total, bound, lean):
    if amount == 2:
        one = jax.random.randint(rng, (), max(1, total - bound), min(bound, total - 1) + 1)
        return jnp.stack([one, total - one])
    lengths = jnp.asarray(length_profile(amount, total, bound, lean), jnp.int32)
    couples = (amount - 1) // 2
    giver, sink = lengths[1:1 + 2 * couples:2], lengths[2:2 + 2 * couples:2]
    margin = jnp.minimum(giver - 1, bound - sink)
    passed = jax.random.randint(jax.random.fold_in(rng, 1), (couples,), 0, 1 << 20) % (margin + 1)
    lengths = lengths.at[1:1 + 2 * couples:2].set(giver - passed).at[2:2 + 2 * couples:2].set(sink + passed)
    return lengths[jax.random.permutation(jax.random.fold_in(rng, 2), amount)]


def setup_inputs(seed: int = 0) -> dict:
    arg_keys = jax.random.split(jax.random.key(seed), 6)
    return {
        "sent_act": draw_sent_act(jax.random.fold_in(arg_keys[5], 71), 0),
        "sent_grad": draw_sent_grad(jax.random.fold_in(arg_keys[5], 71), 0),
        "evicted": draw_evicted(jax.random.fold_in(arg_keys[5], 71), 0),
        "layer_params": draw_layer_params(jax.random.fold_in(arg_keys[5], 71), 0),
        "doc_ids": jax.vmap(lambda own: jnp.searchsorted(jnp.cumsum(uneven_parts(own, SEGS, TOK, TOK // 2, 2)), jnp.arange(TOK), side="right"))(jax.random.split(arg_keys[4], N_DP * N_PIPE * 2)).reshape((N_DP, N_PIPE, 2, TOK)).astype(jnp.int32),
    }


EPS = 1e-05

def normalize(block):
    values = block.astype(jnp.float32)
    centred = values - lax.optimization_barrier(jnp.mean(values, -1, keepdims=True))
    spread = lax.optimization_barrier(jnp.mean(centred * centred, -1, keepdims=True))
    scaling = lax.rsqrt(spread + EPS)
    return (centred * scaling, scaling, values)

def split_heads(block):
    return block.reshape(block.shape[0], -1, HEAD).transpose(1, 0, 2)

def join_heads(block):
    return block.transpose(1, 0, 2).reshape(block.shape[1], -1)

def project(unit, params):
    hidden = unit * params[0]
    query = (hidden * params[1]).astype(jnp.bfloat16)
    keyed = (hidden * params[2]).astype(jnp.bfloat16)
    valued = hidden.astype(jnp.bfloat16)
    return (hidden, split_heads(query), split_heads(keyed), split_heads(valued))

def probabilities(query, keyed, docs):
    scores = jnp.einsum('htd,hsd->hts', query.astype(jnp.float32), keyed.astype(jnp.float32)) * HEAD ** (-0.5)
    position = jnp.arange(docs.shape[0])
    allowed = (position[None, :] <= position[:, None]) & (docs[None, :] == docs[:, None])
    scores = jnp.where(allowed[None], scores, -1e+30)
    peak = lax.optimization_barrier(jnp.max(scores, -1, keepdims=True))
    weights = jnp.exp(scores - peak)
    return weights / lax.optimization_barrier(jnp.sum(weights, -1, keepdims=True))

def section_pass(fwd_block, bwd_block, upstream, docs, params):
    unit, scaling, values = normalize(fwd_block)
    hidden, query, keyed, valued = project(unit, params)
    probs = probabilities(query, keyed, docs[0])
    probs16 = probs.astype(jnp.bfloat16)
    mixed = jnp.einsum('hts,hsd->htd', probs16.astype(jnp.float32), valued.astype(jnp.float32))
    new_act = (values + join_heads(mixed)).astype(jnp.bfloat16)
    unit, scaling, values = normalize(bwd_block)
    hidden, query, keyed, valued = project(unit, params)
    probs = probabilities(query, keyed, docs[1])
    probs16 = probs.astype(jnp.bfloat16)
    grad_heads = split_heads(upstream).astype(jnp.float32)
    grad_vals = jnp.einsum('hts,htd->hsd', probs16.astype(jnp.float32), grad_heads)
    grad_probs = jnp.einsum('htd,hsd->hts', grad_heads, valued.astype(jnp.float32))
    centre = lax.optimization_barrier(jnp.sum(grad_probs * probs, -1, keepdims=True))
    grad_scores = (probs * (grad_probs - centre)).astype(jnp.bfloat16).astype(jnp.float32)
    grad_query = jnp.einsum('hts,hsd->htd', grad_scores, keyed.astype(jnp.float32)) * HEAD ** (-0.5)
    grad_keys = jnp.einsum('hts,htd->hsd', grad_scores, query.astype(jnp.float32)) * HEAD ** (-0.5)
    grad_query = join_heads(grad_query)
    grad_keys = join_heads(grad_keys)
    grad_hidden = grad_query * params[1] + grad_keys * params[2] + join_heads(grad_vals)
    grad_unit = grad_hidden * params[0]
    mean_grad = lax.optimization_barrier(jnp.mean(grad_unit, -1, keepdims=True))
    mean_cross = lax.optimization_barrier(jnp.mean(grad_unit * unit, -1, keepdims=True))
    new_grad = (scaling * (grad_unit - mean_grad - unit * mean_cross) + upstream.astype(jnp.float32)).astype(jnp.bfloat16)
    section_grad = jnp.stack([lax.optimization_barrier(jnp.sum(grad_hidden * unit, 0)), lax.optimization_barrier(jnp.sum(grad_query * hidden, 0)), lax.optimization_barrier(jnp.sum(grad_keys * hidden, 0))])
    return (new_act, new_grad, section_grad)

def flatten_pairs(array):
    return array.reshape((N_DP * N_PIPE,) + array.shape[2:])

def run_item(item):
    return section_pass(item[0], item[1], item[2], item[3], item[4])

def reference(sent_act, sent_grad, evicted, layer_params, doc_ids):
    sections = jnp.arange(N_PIPE).astype(jnp.int32)
    fwd_in = jnp.take(sent_act, (sections - 1) % N_PIPE, axis=1)
    up_grad = jnp.take(sent_grad, (sections + 1) % N_PIPE, axis=1)
    bwd_in = jnp.take(evicted, N_PIPE - 1 - sections, axis=1)
    kept_input = jnp.take(fwd_in, N_PIPE - 1 - sections, axis=1)
    params = jnp.broadcast_to(layer_params[None], (N_DP,) + layer_params.shape)
    results = lax.map(run_item, (flatten_pairs(fwd_in), flatten_pairs(bwd_in), flatten_pairs(up_grad), flatten_pairs(doc_ids), flatten_pairs(params)))
    new_act = results[0].reshape(sent_act.shape)
    new_grad = results[1].reshape(sent_act.shape)
    param_grad = lax.optimization_barrier(jnp.sum(results[2].reshape((N_DP, N_PIPE) + layer_params.shape[1:]), 0))
    return (new_act, new_grad, kept_input, param_grad)
```

```python
import jax
import jax.numpy as jnp
from jax import lax
from jax.experimental import pallas as pl
from jax.experimental.pallas import tpu as pltpu
from jax.sharding import PartitionSpec as P

D = 12288
HEAD = 128
TOK = 256
N_TENSOR = 8
WIDTH = D // N_TENSOR
HEADS = WIDTH // HEAD
SCALE = HEAD ** (-0.5)
EPS = 1e-05
ACT, STASH = 0, 16
F32 = jnp.float32
BF16 = jnp.bfloat16


def move(block, route):
    count = lax.axis_size("pipe")
    return lax.ppermute(block, "pipe", [(j, route(j) % count) for j in range(count)])


def dot(left, right, dims):
    return lax.dot_general(left, right, (dims, ((), ())), preferred_element_type=F32)


def as_rows(first, second):
    lane = lax.broadcasted_iota(jnp.int32, (TOK, HEAD), 1)
    return jnp.transpose(jnp.where(lane == 0, first, second))[0:8]


def as_columns(first, second):
    row = lax.broadcasted_iota(jnp.int32, (HEAD, TOK), 0)
    both = jnp.transpose(jnp.where(row == 0, first, second))
    return both[:, 0:1], both[:, 1:2]


def stats_kernel(place_ref, act_ref, stash_ref, out_ref):
    place = place_ref[0]
    row = lax.broadcasted_iota(jnp.int32, (N_TENSOR, TOK), 0)
    for ref, start in ((act_ref, ACT), (stash_ref, STASH)):
        total = jnp.zeros((TOK, HEAD), F32)
        for h in range(HEADS):
            total = total + ref[:, h * HEAD:(h + 1) * HEAD].astype(F32)
        total = jnp.sum(total, 1, keepdims=True)
        mean = total / WIDTH
        spread = jnp.zeros((TOK, HEAD), F32)
        for h in range(HEADS):
            centred = ref[:, h * HEAD:(h + 1) * HEAD].astype(F32) - mean
            spread = spread + centred * centred
        rows = as_rows(total, jnp.sum(spread, 1, keepdims=True))
        out_ref[start:start + 8] = jnp.where(row == place, rows[0:1], 0.0)
        out_ref[start + 8:start + 16] = jnp.where(row == place, rows[1:2], 0.0)


def local_stats(place, act, stash):
    return pl.pallas_call(
        stats_kernel,
        in_specs=[pl.BlockSpec(memory_space=pltpu.SMEM)] + [pl.BlockSpec(memory_space=pltpu.VMEM)] * 2,
        out_specs=pl.BlockSpec(memory_space=pltpu.VMEM),
        out_shape=jax.ShapeDtypeStruct((4 * N_TENSOR, TOK), F32),
        cost_estimate=pl.CostEstimate(flops=8 * TOK * WIDTH, bytes_accessed=4 * TOK * WIDTH, transcendentals=0),
        compiler_params=pltpu.CompilerParams(vmem_limit_bytes=16 * 2**20),
        name="local_stats",
    )(place, act, stash)


def mean_and_scaling(stats_ref, start):
    sums, squares = stats_ref[start:start + 8], stats_ref[start + 8:start + 16]
    mean = jnp.sum(sums, 0, keepdims=True) / D
    apart = sums / WIDTH - mean
    spread = (jnp.sum(squares, 0, keepdims=True) + WIDTH * jnp.sum(apart * apart, 0, keepdims=True)) / D
    return as_columns(mean, lax.rsqrt(spread + EPS))


def prepare(start, stats_ref, docs_ref, mean_ref, scaling_ref, bias_ref):
    mean, scaling = mean_and_scaling(stats_ref, start)
    mean_ref[...] = jnp.broadcast_to(mean, (TOK, HEAD))
    scaling_ref[...] = jnp.broadcast_to(scaling, (TOK, HEAD))
    docs = docs_ref[...].astype(F32)
    column, _ = as_columns(docs, docs)
    t = lax.broadcasted_iota(jnp.int32, (TOK, TOK), 0)
    u = lax.broadcasted_iota(jnp.int32, (TOK, TOK), 1)
    bias_ref[...] = jnp.where((u <= t) & (column == docs), 0.0, -1e30)


def project(values, mean_ref, scaling_ref, params):
    unit = (values - mean_ref[...]) * scaling_ref[...]
    hidden = unit * params[0:1]
    query = (hidden * params[1:2]).astype(BF16)
    keyed = (hidden * params[2:3]).astype(BF16)
    return unit, hidden, query, keyed, hidden.astype(BF16)


def probabilities(query, keyed, bias_ref):
    scores = dot(query, keyed, ((1,), (1,))) * SCALE + bias_ref[...]
    weights = jnp.exp(scores - jnp.max(scores, 1, keepdims=True))
    return weights * (1.0 / jnp.sum(weights, 1, keepdims=True))


def forward_kernel(stats_ref, docs_ref, params_ref, x_ref, out_ref, mean_ref, scaling_ref, bias_ref):
    @pl.when(pl.program_id(0) == 0)
    def _():
        prepare(ACT, stats_ref, docs_ref, mean_ref, scaling_ref, bias_ref)

    for i in range(x_ref.shape[1] // HEAD):
        part = slice(i * HEAD, (i + 1) * HEAD)
        values = x_ref[:, part].astype(F32)
        _, _, query, keyed, valued = project(values, mean_ref, scaling_ref, params_ref[:, part])
        probs = probabilities(query, keyed, bias_ref).astype(BF16)
        out_ref[:, part] = (values + dot(probs, valued, ((1,), (0,)))).astype(BF16)


def backward_kernel(
    stats_ref, docs_ref, params_ref, x_ref, g_ref, unit_ref, sums_ref, section_ref,
    mean_ref, scaling_ref, bias_ref, sum_ref, cross_ref,
):
    step = pl.program_id(0)

    @pl.when(step == 0)
    def _():
        prepare(STASH, stats_ref, docs_ref, mean_ref, scaling_ref, bias_ref)
        sum_ref[...] = jnp.zeros_like(sum_ref)
        cross_ref[...] = jnp.zeros_like(cross_ref)

    for i in range(x_ref.shape[1] // HEAD):
        part = slice(i * HEAD, (i + 1) * HEAD)
        params = params_ref[:, part]
        unit, hidden, query, keyed, valued = project(x_ref[:, part].astype(F32), mean_ref, scaling_ref, params)
        probs = probabilities(query, keyed, bias_ref)
        g = g_ref[:, part]
        grad_vals = dot(probs.astype(BF16), g, ((0,), (0,)))
        grad_probs = dot(g, valued, ((1,), (1,)))
        centre = jnp.sum(grad_probs * probs, 1, keepdims=True)
        grad_scores = (probs * (grad_probs - centre)).astype(BF16)
        grad_query = dot(grad_scores, keyed, ((1,), (0,))) * SCALE
        grad_keys = dot(grad_scores, query, ((0,), (0,))) * SCALE
        grad_hidden = grad_query * params[1:2] + grad_keys * params[2:3] + grad_vals
        grad_unit = grad_hidden * params[0:1]
        unit_ref[:, part] = grad_unit
        sum_ref[...] += grad_unit
        cross_ref[...] += grad_unit * unit
        section_ref[0:1, part] = jnp.sum(grad_hidden * unit, 0, keepdims=True)
        section_ref[1:2, part] = jnp.sum(grad_query * hidden, 0, keepdims=True)
        section_ref[2:3, part] = jnp.sum(grad_keys * hidden, 0, keepdims=True)

    @pl.when(step == pl.num_programs(0) - 1)
    def _():
        sums_ref[...] = as_rows(
            jnp.sum(sum_ref[...], 1, keepdims=True), jnp.sum(cross_ref[...], 1, keepdims=True)
        )


def result_kernel(stats_ref, sums_ref, x_ref, g_ref, unit_ref, out_ref):
    mean, scaling = mean_and_scaling(stats_ref, STASH)
    mean_grad, mean_cross = as_columns(sums_ref[0:1] / D, sums_ref[1:2] / D)
    for i in range(x_ref.shape[1] // HEAD):
        part = slice(i * HEAD, (i + 1) * HEAD)
        unit = (x_ref[:, part].astype(F32) - mean) * scaling
        inner = unit_ref[:, part] - mean_grad - unit * mean_cross
        out_ref[:, part] = (scaling * inner + g_ref[:, part].astype(F32)).astype(BF16)


def whole(shape):
    return pl.BlockSpec(shape, lambda i: (0, 0))


def columns(rows, heads):
    return pl.BlockSpec((rows, heads * HEAD), lambda i: (0, i))


def forward_layer(stats, docs, params, block, heads=2):
    return pl.pallas_call(
        forward_kernel,
        grid=(HEADS // heads,),
        in_specs=[whole((32, TOK)), whole((1, TOK)), columns(3, heads), columns(TOK, heads)],
        out_specs=columns(TOK, heads),
        out_shape=jax.ShapeDtypeStruct((TOK, WIDTH), BF16),
        scratch_shapes=[pltpu.VMEM((TOK, HEAD), F32)] * 2 + [pltpu.VMEM((TOK, TOK), F32)],
        cost_estimate=pl.CostEstimate(
            flops=4 * HEADS * TOK * TOK * HEAD, bytes_accessed=4 * TOK * WIDTH, transcendentals=HEADS * TOK * TOK
        ),
        compiler_params=pltpu.CompilerParams(vmem_limit_bytes=24 * 2**20),
        name="forward_layer",
    )(stats, docs, params, block)


def backward_layer(stats, docs, params, block, upstream, heads=2):
    return pl.pallas_call(
        backward_kernel,
        grid=(HEADS // heads,),
        in_specs=[whole((32, TOK)), whole((1, TOK)), columns(3, heads), columns(TOK, heads), columns(TOK, heads)],
        out_specs=[columns(TOK, heads), whole((8, TOK)), columns(3, heads)],
        out_shape=[
            jax.ShapeDtypeStruct((TOK, WIDTH), F32),
            jax.ShapeDtypeStruct((8, TOK), F32),
            jax.ShapeDtypeStruct((3, WIDTH), F32),
        ],
        scratch_shapes=[pltpu.VMEM((TOK, HEAD), F32)] * 2
        + [pltpu.VMEM((TOK, TOK), F32)]
        + [pltpu.VMEM((TOK, HEAD), F32)] * 2,
        cost_estimate=pl.CostEstimate(
            flops=10 * HEADS * TOK * TOK * HEAD, bytes_accessed=8 * TOK * WIDTH, transcendentals=HEADS * TOK * TOK
        ),
        compiler_params=pltpu.CompilerParams(vmem_limit_bytes=24 * 2**20),
        name="backward_layer",
    )(stats, docs, params, block, upstream)


def result_layer(stats, sums, block, upstream, grad_unit, heads=3):
    return pl.pallas_call(
        result_kernel,
        grid=(HEADS // heads,),
        in_specs=[whole((32, TOK)), whole((8, TOK))] + [columns(TOK, heads)] * 3,
        out_specs=columns(TOK, heads),
        out_shape=jax.ShapeDtypeStruct((TOK, WIDTH), BF16),
        cost_estimate=pl.CostEstimate(flops=8 * TOK * WIDTH, bytes_accessed=10 * TOK * WIDTH, transcendentals=0),
        compiler_params=pltpu.CompilerParams(vmem_limit_bytes=24 * 2**20),
        name="result_layer",
    )(stats, sums, block, upstream, grad_unit)


def local(sent_act, sent_grad, evicted, layer_params, doc_ids):
    act, grad, stash = sent_act[0, 0], sent_grad[0, 0], evicted[0, 0]
    params, docs = layer_params[0], doc_ids[0, 0]
    place = lax.axis_index("tensor").astype(jnp.int32).reshape(1)

    bwd_in = move(stash, lambda j: 15 - j)
    up_grad = move(grad, lambda j: j - 1)
    fwd_in = move(act, lambda j: j + 1)
    stats = lax.psum(local_stats(place, act, stash), "tensor")
    bwd_stats = move(stats, lambda j: 15 - j)
    fwd_stats = move(stats, lambda j: j + 1)
    kept_input = move(act, lambda j: 14 - j)

    new_act = forward_layer(fwd_stats, docs[0:1], params, fwd_in)
    grad_unit, sums, section_grad = backward_layer(bwd_stats, docs[1:2], params, bwd_in, up_grad)
    sums = lax.psum(sums, "tensor")
    new_grad = result_layer(bwd_stats, sums, bwd_in, up_grad, grad_unit)
    summed = jnp.sum(lax.all_gather(section_grad, "dp"), 0)
    return (new_act[None, None], new_grad[None, None], kept_input[None, None], summed[None])


def solution(mesh):
    blocks = P("dp", "pipe", None, "tensor")
    weights = P("pipe", None, "tensor")
    return jax.shard_map(
        local,
        mesh=mesh,
        in_specs=(blocks, blocks, blocks, weights, P("dp", "pipe", None, None)),
        out_specs=(blocks, blocks, blocks, weights),
        check_vma=False,
    )
```

```python
import functools

import jax
import jax.numpy as jnp
from jax import lax
from jax.experimental import pallas as pl
from jax.experimental.pallas import tpu as pltpu
from jax.sharding import PartitionSpec as P

D = 12288
HEAD = 128
TOK = 256
N_TENSOR = 8
WIDTH = D // N_TENSOR
HEADS = WIDTH // HEAD
SCALE = HEAD ** (-0.5)
EPS = 1e-05
LOG2E = 1.4426950408889634
PIECES = 4
SUM, SQUARES, CROSS, GRAD = 0, 1, 2, 3
F32 = jnp.float32
BF16 = jnp.bfloat16
VMEM = 56 * 2**20


def move(block, route):
    count = lax.axis_size("pipe")
    pairs = [(j, route(j) % count) for j in range(count) if route(j) is not None]
    return lax.ppermute(block, "pipe", pairs)


def dot(left, right, dims):
    return lax.dot_general(left, right, (dims, ((), ())), preferred_element_type=F32)


def as_rows(*columns):
    lane = lax.broadcasted_iota(jnp.int32, (TOK, HEAD), 1)
    packed = jnp.broadcast_to(columns[-1], (TOK, HEAD))
    for i in range(len(columns) - 2, -1, -1):
        packed = jnp.where(lane <= i, columns[i], packed)
    return jnp.transpose(packed)[0:8]


def as_columns(first, second):
    row = lax.broadcasted_iota(jnp.int32, (HEAD, TOK), 0)
    both = jnp.transpose(jnp.where(row == 0, first, second))
    return both[:, 0:1], both[:, 1:2]


def to_all(out_ref, rows):
    for i in range(N_TENSOR):
        out_ref[8 * i:8 * i + 8] = rows


def from_all(ref, row):
    return [ref[8 * i + row:8 * i + row + 1] for i in range(N_TENSOR)]


class Spread:
    def __init__(self, pivot_ref, sum_ref, square_ref):
        self.pivot, self.sum, self.square = pivot_ref, sum_ref, square_ref

    def first(self, piece):
        self.pivot[...] = jnp.broadcast_to(jnp.sum(piece, 1, keepdims=True) / HEAD, (TOK, HEAD))
        self.sum[...] = jnp.zeros_like(self.sum)
        self.square[...] = jnp.zeros_like(self.square)

    def add(self, piece):
        away = piece - self.pivot[...]
        self.sum[...] += away
        self.square[...] += away * away

    def result(self):
        away = jnp.sum(self.sum[...], 1, keepdims=True)
        square = jnp.sum(self.square[...], 1, keepdims=True)
        return away + WIDTH * self.pivot[:, 0:1], square - away * away / WIDTH


def stats_kernel(*refs):
    pieces, out_ref, scratch = refs[:PIECES], refs[PIECES], refs[PIECES + 1:]
    spread = Spread(*scratch)
    spread.first(pieces[0][:, 0:HEAD].astype(F32))
    for ref in pieces:
        for i in range(ref.shape[1] // HEAD):
            spread.add(ref[:, i * HEAD:(i + 1) * HEAD].astype(F32))
    to_all(out_ref, as_rows(*spread.result()))


def local_stats(block):
    pieces = [pl.BlockSpec((TOK, WIDTH // PIECES), functools.partial(lambda p, i: (0, p), p)) for p in range(PIECES)]
    return pl.pallas_call(
        stats_kernel,
        grid=(1,),
        in_specs=pieces,
        out_specs=whole((64, TOK)),
        out_shape=jax.ShapeDtypeStruct((8 * N_TENSOR, TOK), F32),
        scratch_shapes=[pltpu.VMEM((TOK, HEAD), F32)] * 3,
        cost_estimate=pl.CostEstimate(flops=8 * TOK * WIDTH, bytes_accessed=2 * TOK * WIDTH, transcendentals=0),
        compiler_params=pltpu.CompilerParams(vmem_limit_bytes=VMEM),
        name="local_stats",
    )(*[block] * PIECES)


def exchange(rows):
    return lax.all_to_all(rows, "tensor", 0, 0, tiled=True)


def mean_and_scaling(stats_ref):
    sums, squares = from_all(stats_ref, SUM), from_all(stats_ref, SQUARES)
    mean = sum(sums) / D
    apart = [piece / WIDTH - mean for piece in sums]
    spread = (sum(squares) + WIDTH * sum(piece * piece for piece in apart)) / D
    return as_columns(mean, lax.rsqrt(spread + EPS))


def prepare(which, stats_ref, docs_ref, mean_ref, scaling_ref, bias_ref):
    mean, scaling = mean_and_scaling(stats_ref)
    mean_ref[...] = jnp.broadcast_to(mean, (TOK, HEAD))
    scaling_ref[...] = jnp.broadcast_to(scaling, (TOK, HEAD))
    docs = docs_ref[which:which + 1].astype(F32)
    column, _ = as_columns(docs, docs)
    t = lax.broadcasted_iota(jnp.int32, (TOK, TOK), 0)
    u = lax.broadcasted_iota(jnp.int32, (TOK, TOK), 1)
    bias_ref[...] = jnp.where((t <= u) & (column == docs), 0.0, -1e30)


def project(values, mean_ref, scaling_ref, params):
    unit = (values - mean_ref[...]) * scaling_ref[...]
    hidden = unit * params[0]
    query = (hidden * params[1]).astype(BF16)
    keyed = (hidden * params[2]).astype(BF16)
    return unit, hidden, query, keyed, hidden.astype(BF16)


def probabilities(query, keyed, bias_ref):
    scores = dot(keyed, query, ((1,), (1,))) * (SCALE * LOG2E) + bias_ref[...]
    weights = jnp.exp2(scores - jnp.max(scores, 0, keepdims=True))
    return weights * (1.0 / jnp.sum(weights, 0, keepdims=True))


def backward_kernel(
    odd_ref, stats_ref, docs_ref, params_ref, x_ref, one_ref, two_ref,
    unit_ref, act_ref, g_ref, sums_ref, section_ref,
    mean_ref, scaling_ref, bias_ref, sum_ref, cross_ref, *scratch
):
    step = pl.program_id(0)
    spread = Spread(*scratch)

    @pl.when(odd_ref[0] == 0)
    def _():
        act_ref[...] = one_ref[...]
        g_ref[...] = two_ref[...]

    @pl.when(odd_ref[0] == 1)
    def _():
        act_ref[...] = two_ref[...]
        g_ref[...] = one_ref[...]

    @pl.when(step == 0)
    def _():
        prepare(1, stats_ref, docs_ref, mean_ref, scaling_ref, bias_ref)
        sum_ref[...] = jnp.zeros_like(sum_ref)
        cross_ref[...] = jnp.zeros_like(cross_ref)
        spread.first(act_ref[:, 0:HEAD].astype(F32))

    for i in range(x_ref.shape[1] // HEAD):
        part = slice(i * HEAD, (i + 1) * HEAD)
        spread.add(act_ref[:, part].astype(F32))
        params = params_ref[:, :, part]
        unit, hidden, query, keyed, valued = project(x_ref[:, part].astype(F32), mean_ref, scaling_ref, params)
        probs = probabilities(query, keyed, bias_ref)
        g = g_ref[:, part]
        grad_vals = dot(probs.astype(BF16), g, ((1,), (0,)))
        grad_probs = dot(valued, g, ((1,), (1,)))
        centre = jnp.sum(grad_probs * probs, 0, keepdims=True)
        grad_scores = (probs * (grad_probs - centre)).astype(BF16)
        grad_query = dot(grad_scores, keyed, ((0,), (0,)))
        grad_keys = dot(grad_scores, query, ((1,), (0,)))
        grad_hidden = grad_query * (params[1] * SCALE) + grad_keys * (params[2] * SCALE) + grad_vals
        grad_unit = grad_hidden * params[0]
        unit_ref[:, part] = grad_unit
        sum_ref[...] += grad_unit
        cross_ref[...] += grad_unit * unit
        section_ref[0, :, part] = jnp.sum(grad_hidden * unit, 0, keepdims=True)
        section_ref[1, :, part] = jnp.sum(grad_query * hidden, 0, keepdims=True) * SCALE
        section_ref[2, :, part] = jnp.sum(grad_keys * hidden, 0, keepdims=True) * SCALE

    @pl.when(step == pl.num_programs(0) - 1)
    def _():
        total, squares = spread.result()
        grad = jnp.sum(sum_ref[...], 1, keepdims=True)
        cross = jnp.sum(cross_ref[...], 1, keepdims=True)
        to_all(sums_ref, as_rows(total, squares, cross, grad))


def finish_kernel(
    stats_ref, sums_ref, docs_ref, params_ref, act_ref, x_ref, g_ref, unit_ref, new_act_ref, new_grad_ref,
    mean_ref, scaling_ref, bias_ref, own_ref,
):
    @pl.when(pl.program_id(0) == 0)
    def _():
        prepare(0, sums_ref, docs_ref, mean_ref, scaling_ref, bias_ref)
        mean, scaling = mean_and_scaling(stats_ref)
        mean_grad, mean_cross = as_columns(
            sum(from_all(sums_ref, GRAD)) / D, sum(from_all(sums_ref, CROSS)) / D
        )
        for i, column in enumerate((mean, scaling, mean_grad, mean_cross)):
            own_ref[i] = jnp.broadcast_to(column, (TOK, HEAD))

    for i in range(x_ref.shape[1] // HEAD):
        part = slice(i * HEAD, (i + 1) * HEAD)
        unit = (x_ref[:, part].astype(F32) - own_ref[0]) * own_ref[1]
        inner = unit_ref[:, part] - own_ref[2] - unit * own_ref[3]
        new_grad_ref[:, part] = (own_ref[1] * inner + g_ref[:, part].astype(F32)).astype(BF16)
        values = act_ref[:, part].astype(F32)
        _, _, query, keyed, valued = project(values, mean_ref, scaling_ref, params_ref[:, :, part])
        probs = probabilities(query, keyed, bias_ref).astype(BF16)
        new_act_ref[:, part] = (values + dot(probs, valued, ((0,), (0,)))).astype(BF16)


def whole(shape):
    return pl.BlockSpec(shape, lambda i: (0, 0))


def columns(rows, heads):
    return pl.BlockSpec((rows, heads * HEAD), lambda i: (0, i))


def layer(heads):
    return pl.BlockSpec((3, 1, heads * HEAD), lambda i: (0, 0, i))


def backward_layer(odd, stats, docs, params, block, one, two, heads=12):
    wide = columns(TOK, heads)
    return pl.pallas_call(
        backward_kernel,
        grid=(HEADS // heads,),
        in_specs=[pl.BlockSpec(memory_space=pltpu.SMEM), whole((64, TOK)), whole((2, TOK)), layer(heads)] + [wide] * 3,
        out_specs=[wide, wide, wide, whole((64, TOK)), layer(heads)],
        out_shape=[
            jax.ShapeDtypeStruct((TOK, WIDTH), F32),
            jax.ShapeDtypeStruct((TOK, WIDTH), BF16),
            jax.ShapeDtypeStruct((TOK, WIDTH), BF16),
            jax.ShapeDtypeStruct((64, TOK), F32),
            jax.ShapeDtypeStruct((3, 1, WIDTH), F32),
        ],
        scratch_shapes=[pltpu.VMEM((TOK, HEAD), F32)] * 2
        + [pltpu.VMEM((TOK, TOK), F32)]
        + [pltpu.VMEM((TOK, HEAD), F32)] * 5,
        cost_estimate=pl.CostEstimate(
            flops=10 * HEADS * TOK * TOK * HEAD, bytes_accessed=14 * TOK * WIDTH, transcendentals=HEADS * TOK * TOK
        ),
        compiler_params=pltpu.CompilerParams(vmem_limit_bytes=VMEM),
        name="backward_layer",
    )(odd, stats, docs, params, block, one, two)


def finish_layer(stats, sums, docs, params, act, block, upstream, grad_unit, heads=12):
    wide = columns(TOK, heads)
    return pl.pallas_call(
        finish_kernel,
        grid=(HEADS // heads,),
        in_specs=[whole((64, TOK)), whole((64, TOK)), whole((2, TOK)), layer(heads)] + [wide] * 4,
        out_specs=[wide, wide],
        out_shape=[jax.ShapeDtypeStruct((TOK, WIDTH), BF16)] * 2,
        scratch_shapes=[pltpu.VMEM((TOK, HEAD), F32)] * 2
        + [pltpu.VMEM((TOK, TOK), F32), pltpu.VMEM((4, TOK, HEAD), F32)],
        cost_estimate=pl.CostEstimate(
            flops=4 * HEADS * TOK * TOK * HEAD, bytes_accessed=14 * TOK * WIDTH, transcendentals=HEADS * TOK * TOK
        ),
        compiler_params=pltpu.CompilerParams(vmem_limit_bytes=VMEM),
        name="finish_layer",
    )(stats, sums, docs, params, act, block, upstream, grad_unit)


def mirror(j):
    return 15 - j


def odd_swap(j):
    return j + 1 if j % 2 else j - 1


def even_swap(j):
    return j - 1 if j % 2 else j + 1


def far(wanted):
    return lambda j: 14 - j if (j % 4 == 1) == wanted else None


def local(sent_act, sent_grad, evicted, layer_params, doc_ids):
    act, grad, stash = sent_act[0, 0], sent_grad[0, 0], evicted[0, 0]
    params, docs = jnp.transpose(layer_params, (1, 0, 2)), doc_ids[0, 0]
    place = lax.axis_index("pipe").astype(jnp.int32)
    odd = place & 1

    bwd_in = move(stash, mirror)
    swapped_odd = move(jnp.where(odd == 1, act, grad), odd_swap)
    swapped_even = move(jnp.where(odd == 1, grad, act), even_swap)

    stats = exchange(local_stats(bwd_in))
    later_act, swapped_odd, swapped_even = lax.optimization_barrier((act, swapped_odd, swapped_even))
    kept_near = move(later_act, far(False))
    grad_unit, fwd_in, up_grad, sums, section_grad = backward_layer(
        odd.reshape(1), stats, docs, params, bwd_in, swapped_odd, swapped_even
    )
    last_act, sums, section_grad = lax.optimization_barrier((act, sums, section_grad))
    kept_far = move(last_act, far(True))
    sums = exchange(sums)
    summed = jnp.transpose(jnp.sum(lax.all_gather(section_grad, "dp"), 0), (1, 0, 2))
    new_act, new_grad = finish_layer(stats, sums, docs, params, fwd_in, bwd_in, up_grad, grad_unit)
    kept_input = jnp.where(place & 3 == 1, kept_far, kept_near)
    return (new_act[None, None], new_grad[None, None], kept_input[None, None], summed)


def solution(mesh):
    blocks = P("dp", "pipe", None, "tensor")
    weights = P("pipe", None, "tensor")
    return jax.shard_map(
        local,
        mesh=mesh,
        in_specs=(blocks, blocks, blocks, weights, P("dp", "pipe", None, None)),
        out_specs=(blocks, blocks, blocks, weights),
        check_vma=False,
    )
```

```python
import jax
import jax.numpy as jnp
from jax import lax
from jax.experimental import pallas as pl
from jax.experimental.pallas import tpu as pltpu
from jax.sharding import PartitionSpec as P

D = 12288
HEAD = 128
HALF = 128
TOK = 256
N_TENSOR = 8
WIDTH = D // N_TENSOR
HEADS = WIDTH // HEAD
SCALE = HEAD ** (-0.5)
EPS = 1e-05
LOG2E = 1.4426950408889634
SUM, SQUARES, CROSS, GRAD = 0, 1, 2, 3
F32 = jnp.float32
BF16 = jnp.bfloat16
VMEM = 56 * 2**20


def move(block, route):
    count = lax.axis_size("pipe")
    pairs = [(j, route(j) % count) for j in range(count) if route(j) is not None]
    return lax.ppermute(block, "pipe", pairs)


def dot(left, right, dims):
    return lax.dot_general(left, right, (dims, ((), ())), preferred_element_type=F32)


def as_rows(*columns):
    lane = lax.broadcasted_iota(jnp.int32, (TOK, HEAD), 1)
    packed = jnp.broadcast_to(columns[-1], (TOK, HEAD))
    for i in range(len(columns) - 2, -1, -1):
        packed = jnp.where(lane <= i, columns[i], packed)
    return jnp.transpose(packed)[0:8]


def as_columns(first, second):
    row = lax.broadcasted_iota(jnp.int32, (HEAD, TOK), 0)
    both = jnp.transpose(jnp.where(row == 0, first, second))
    return both[:, 0:1], both[:, 1:2]


def to_all(out_ref, rows):
    for i in range(N_TENSOR):
        out_ref[8 * i:8 * i + 8] = rows


def from_all(ref, row):
    return [ref[8 * i + row:8 * i + row + 1] for i in range(N_TENSOR)]


class Spread:
    def __init__(self, pivot_ref, sum_ref, square_ref):
        self.pivot, self.sum, self.square = pivot_ref, sum_ref, square_ref

    def first(self, piece):
        self.pivot[...] = jnp.broadcast_to(jnp.sum(piece, 1, keepdims=True) / HEAD, (TOK, HEAD))
        self.sum[...] = jnp.zeros_like(self.sum)
        self.square[...] = jnp.zeros_like(self.square)

    def add(self, piece):
        away = piece - self.pivot[...]
        self.sum[...] += away
        self.square[...] += away * away

    def result(self):
        away = jnp.sum(self.sum[...], 1, keepdims=True)
        square = jnp.sum(self.square[...], 1, keepdims=True)
        return away + WIDTH * self.pivot[:, 0:1], square - away * away / WIDTH


def stats_kernel(x_ref, out_ref, *scratch):
    spread = Spread(*scratch)
    spread.first(x_ref[:, 0:HEAD].astype(F32))
    for h in range(HEADS):
        spread.add(x_ref[:, h * HEAD:(h + 1) * HEAD].astype(F32))
    to_all(out_ref, as_rows(*spread.result()))


def local_stats(block):
    return pl.pallas_call(
        stats_kernel,
        in_specs=[pl.BlockSpec(memory_space=pltpu.VMEM)],
        out_specs=pl.BlockSpec(memory_space=pltpu.VMEM),
        out_shape=jax.ShapeDtypeStruct((8 * N_TENSOR, TOK), F32),
        scratch_shapes=[pltpu.VMEM((TOK, HEAD), F32)] * 3,
        cost_estimate=pl.CostEstimate(flops=8 * TOK * WIDTH, bytes_accessed=2 * TOK * WIDTH, transcendentals=0),
        compiler_params=pltpu.CompilerParams(vmem_limit_bytes=16 * 2**20),
        name="local_stats",
    )(block)


def exchange(rows):
    return lax.all_to_all(rows, "tensor", 0, 0, tiled=True)


def mean_and_scaling(stats_ref):
    sums, squares = from_all(stats_ref, SUM), from_all(stats_ref, SQUARES)
    mean = sum(sums) / D
    apart = [piece / WIDTH - mean for piece in sums]
    spread = (sum(squares) + WIDTH * sum(piece * piece for piece in apart)) / D
    return as_columns(mean, lax.rsqrt(spread + EPS))


def prepare(which, stats_ref, docs_ref, mean_ref, scaling_ref, bias_ref):
    mean, scaling = mean_and_scaling(stats_ref)
    mean_ref[...] = jnp.broadcast_to(mean, (TOK, HEAD))
    scaling_ref[...] = jnp.broadcast_to(scaling, (TOK, HEAD))
    docs = docs_ref[which:which + 1].astype(F32)
    column, _ = as_columns(docs, docs)
    t = lax.broadcasted_iota(jnp.int32, (TOK, TOK), 0)
    u = lax.broadcasted_iota(jnp.int32, (TOK, TOK), 1)
    bias_ref[...] = jnp.where((t <= u) & (column == docs), 0.0, -1e30)


def project(values, mean_ref, scaling_ref, params):
    unit = (values - mean_ref[...]) * scaling_ref[...]
    hidden = unit * params[0]
    query = (hidden * params[1]).astype(BF16)
    keyed = (hidden * params[2]).astype(BF16)
    return unit, hidden, query, keyed, hidden.astype(BF16)


def probabilities(query, keyed, bias_ref):
    scores = dot(keyed, query, ((1,), (1,))) * (SCALE * LOG2E) + bias_ref[...]
    weights = jnp.exp2(scores - jnp.max(scores, 0, keepdims=True))
    return weights * (1.0 / jnp.sum(weights, 0, keepdims=True))


def backward_kernel(
    odd_ref, stats_ref, docs_ref, params_ref, x_ref, one_ref, two_ref,
    unit_ref, act_ref, g_ref, sums_ref, section_ref,
    mean_ref, scaling_ref, bias_ref, sum_ref, cross_ref, *scratch
):
    step = pl.program_id(0)
    spread = Spread(*scratch)

    @pl.when(odd_ref[0] == 0)
    def _():
        act_ref[...] = one_ref[...]
        g_ref[...] = two_ref[...]

    @pl.when(odd_ref[0] == 1)
    def _():
        act_ref[...] = two_ref[...]
        g_ref[...] = one_ref[...]

    @pl.when(step == 0)
    def _():
        prepare(1, stats_ref, docs_ref, mean_ref, scaling_ref, bias_ref)
        sum_ref[...] = jnp.zeros_like(sum_ref)
        cross_ref[...] = jnp.zeros_like(cross_ref)
        spread.first(act_ref[:, 0:HEAD].astype(F32))

    for i in range(x_ref.shape[1] // HEAD):
        part = slice(i * HEAD, (i + 1) * HEAD)
        spread.add(act_ref[:, part].astype(F32))
        params = params_ref[:, :, part]
        unit, hidden, query, keyed, valued = project(x_ref[:, part].astype(F32), mean_ref, scaling_ref, params)
        probs = probabilities(query, keyed, bias_ref)
        g = g_ref[:, part]
        grad_vals = dot(probs.astype(BF16), g, ((1,), (0,)))
        grad_probs = dot(valued, g, ((1,), (1,)))
        centre = jnp.sum(grad_probs * probs, 0, keepdims=True)
        grad_scores = (probs * (grad_probs - centre)).astype(BF16)
        grad_query = dot(grad_scores, keyed, ((0,), (0,)))
        grad_keys = dot(grad_scores, query, ((1,), (0,)))
        grad_hidden = grad_query * (params[1] * SCALE) + grad_keys * (params[2] * SCALE) + grad_vals
        grad_unit = grad_hidden * params[0]
        unit_ref[:, part] = grad_unit
        sum_ref[...] += grad_unit
        cross_ref[...] += grad_unit * unit
        section_ref[0, :, part] = jnp.sum(grad_hidden * unit, 0, keepdims=True)
        section_ref[1, :, part] = jnp.sum(grad_query * hidden, 0, keepdims=True)
        section_ref[2, :, part] = jnp.sum(grad_keys * hidden, 0, keepdims=True)

    @pl.when(step == pl.num_programs(0) - 1)
    def _():
        total, squares = spread.result()
        grad = jnp.sum(sum_ref[...], 1, keepdims=True)
        cross = jnp.sum(cross_ref[...], 1, keepdims=True)
        to_all(sums_ref, as_rows(total, squares, cross, grad))


def finish_kernel(
    stats_ref, sums_ref, docs_ref, params_ref, act_ref, x_ref, g_ref, unit_ref, new_act_ref, new_grad_ref,
    mean_ref, scaling_ref, bias_ref, own_ref,
):
    @pl.when(pl.program_id(0) == 0)
    def _():
        prepare(0, sums_ref, docs_ref, mean_ref, scaling_ref, bias_ref)
        mean, scaling = mean_and_scaling(stats_ref)
        mean_grad, mean_cross = as_columns(
            sum(from_all(sums_ref, GRAD)) / D, sum(from_all(sums_ref, CROSS)) / D
        )
        for i, column in enumerate((mean, scaling, mean_grad, mean_cross)):
            own_ref[i] = jnp.broadcast_to(column, (TOK, HEAD))

    for i in range(x_ref.shape[1] // HEAD):
        part = slice(i * HEAD, (i + 1) * HEAD)
        unit = (x_ref[:, part].astype(F32) - own_ref[0]) * own_ref[1]
        inner = unit_ref[:, part] - own_ref[2] - unit * own_ref[3]
        new_grad_ref[:, part] = (own_ref[1] * inner + g_ref[:, part].astype(F32)).astype(BF16)
        values = act_ref[:, part].astype(F32)
        _, _, query, keyed, valued = project(values, mean_ref, scaling_ref, params_ref[:, :, part])
        probs = probabilities(query, keyed, bias_ref).astype(BF16)
        new_act_ref[:, part] = (values + dot(probs, valued, ((0,), (0,)))).astype(BF16)


def whole(shape):
    return pl.BlockSpec(shape, lambda i: (0, 0))


def columns(rows, heads):
    return pl.BlockSpec((rows, heads * HEAD), lambda i: (0, i))


def layer(heads):
    return pl.BlockSpec((3, 1, heads * HEAD), lambda i: (0, 0, i))


def backward_layer(odd, stats, docs, params, block, one, two, heads=12):
    wide = columns(TOK, heads)
    return pl.pallas_call(
        backward_kernel,
        grid=(HEADS // heads,),
        in_specs=[pl.BlockSpec(memory_space=pltpu.SMEM), whole((64, TOK)), whole((2, TOK)), layer(heads)] + [wide] * 3,
        out_specs=[wide, wide, wide, whole((64, TOK)), layer(heads)],
        out_shape=[
            jax.ShapeDtypeStruct((TOK, WIDTH), F32),
            jax.ShapeDtypeStruct((TOK, WIDTH), BF16),
            jax.ShapeDtypeStruct((TOK, WIDTH), BF16),
            jax.ShapeDtypeStruct((64, TOK), F32),
            jax.ShapeDtypeStruct((3, 1, WIDTH), F32),
        ],
        scratch_shapes=[pltpu.VMEM((TOK, HEAD), F32)] * 2
        + [pltpu.VMEM((TOK, TOK), F32)]
        + [pltpu.VMEM((TOK, HEAD), F32)] * 5,
        cost_estimate=pl.CostEstimate(
            flops=10 * HEADS * TOK * TOK * HEAD, bytes_accessed=14 * TOK * WIDTH, transcendentals=HEADS * TOK * TOK
        ),
        compiler_params=pltpu.CompilerParams(vmem_limit_bytes=VMEM),
        name="backward_layer",
    )(odd, stats, docs, params, block, one, two)


def scaled_kernel(in_ref, out_ref):
    out_ref[0] = in_ref[0]
    out_ref[1] = in_ref[1] * SCALE
    out_ref[2] = in_ref[2] * SCALE


def scaled(section_grad):
    return pl.pallas_call(
        scaled_kernel,
        out_shape=jax.ShapeDtypeStruct((3, 1, WIDTH), F32),
        cost_estimate=pl.CostEstimate(flops=2 * 10**10, bytes_accessed=24 * WIDTH, transcendentals=0),
        name="scaled_section_grad",
    )(section_grad)


def finish_layer(stats, sums, docs, params, act, block, upstream, grad_unit, heads=12):
    wide = columns(TOK, heads)
    return pl.pallas_call(
        finish_kernel,
        grid=(HEADS // heads,),
        in_specs=[whole((64, TOK)), whole((64, TOK)), whole((2, TOK)), layer(heads)] + [wide] * 4,
        out_specs=[wide, wide],
        out_shape=[jax.ShapeDtypeStruct((TOK, WIDTH), BF16)] * 2,
        scratch_shapes=[pltpu.VMEM((TOK, HEAD), F32)] * 2
        + [pltpu.VMEM((TOK, TOK), F32), pltpu.VMEM((4, TOK, HEAD), F32)],
        cost_estimate=pl.CostEstimate(
            flops=4 * HEADS * TOK * TOK * HEAD, bytes_accessed=14 * TOK * WIDTH, transcendentals=HEADS * TOK * TOK
        ),
        compiler_params=pltpu.CompilerParams(vmem_limit_bytes=VMEM),
        name="finish_layer",
    )(stats, sums, docs, params, act, block, upstream, grad_unit)


def mirror(j):
    return 15 - j


def odd_swap(j):
    return j + 1 if j % 2 else j - 1


def even_swap(j):
    return j - 1 if j % 2 else j + 1


def near(j):
    return 14 - j if j % 4 != 1 else None


def far(j):
    return 14 - j if j % 4 == 1 else None


def relay_in(j):
    return j + 2 if j % 4 == 1 else None


def relay_out(j):
    return 16 - j if j % 4 == 3 else None


def local(sent_act, sent_grad, evicted, layer_params, doc_ids):
    act, grad, stash = sent_act[0, 0], sent_grad[0, 0], evicted[0, 0]
    params, docs = jnp.transpose(layer_params, (1, 0, 2)), doc_ids[0, 0]
    place = lax.axis_index("pipe").astype(jnp.int32)
    odd = place & 1

    bwd_in = move(stash, mirror)
    swapped_odd = move(jnp.where(odd == 1, act, grad), odd_swap)
    swapped_even = move(jnp.where(odd == 1, grad, act), even_swap)

    relayed = move(act[HALF:], relay_in)
    stats = exchange(local_stats(bwd_in))
    later_act, swapped_odd, swapped_even = lax.optimization_barrier((act, swapped_odd, swapped_even))
    kept_near = move(later_act, near)
    relayed = move(relayed, relay_out)
    grad_unit, fwd_in, up_grad, sums, section_grad = backward_layer(
        odd.reshape(1), stats, docs, params, bwd_in, swapped_odd, swapped_even
    )
    sums = exchange(sums)
    gathered = lax.all_gather(scaled(section_grad), "dp")
    sums, gathered = lax.optimization_barrier((sums, gathered))
    new_act, new_grad = finish_layer(stats, sums, docs, params, fwd_in, bwd_in, up_grad, grad_unit)
    last_act, new_grad = lax.optimization_barrier((act[:HALF], new_grad))
    kept_far = move(last_act, far)
    summed = jnp.transpose(jnp.sum(gathered, 0), (1, 0, 2))
    kept_input = jnp.where(place & 3 == 1, jnp.concatenate([kept_far, relayed], 0), kept_near)
    return (new_act[None, None], new_grad[None, None], kept_input[None, None], summed)


def solution(mesh):
    blocks = P("dp", "pipe", None, "tensor")
    weights = P("pipe", None, "tensor")
    return jax.shard_map(
        local,
        mesh=mesh,
        in_specs=(blocks, blocks, blocks, weights, P("dp", "pipe", None, None)),
        out_specs=(blocks, blocks, blocks, weights),
        check_vma=False,
    )
```

```python
import jax
import jax.numpy as jnp
from jax import lax
from jax.experimental import pallas as pl
from jax.experimental.pallas import tpu as pltpu
from jax.sharding import PartitionSpec as P

D = 12288
HEAD = 128
HALF = 128
TOK = 256
N_TENSOR = 8
N_DP = 4
WIDTH = D // N_TENSOR
HEADS = WIDTH // HEAD
SCALE = HEAD ** (-0.5)
EPS = 1e-05
LOG2E = 1.4426950408889634
SUM, SQUARES, CROSS, GRAD = 0, 1, 2, 3
F32 = jnp.float32
BF16 = jnp.bfloat16
VMEM = 56 * 2**20


def move(block, route):
    count = lax.axis_size("pipe")
    pairs = [(j, route(j) % count) for j in range(count) if route(j) is not None]
    return lax.ppermute(block, "pipe", pairs)


def dot(left, right, dims):
    return lax.dot_general(left, right, (dims, ((), ())), preferred_element_type=F32)


def as_rows(*columns):
    lane = lax.broadcasted_iota(jnp.int32, (TOK, HEAD), 1)
    packed = jnp.broadcast_to(columns[-1], (TOK, HEAD))
    for i in range(len(columns) - 2, -1, -1):
        packed = jnp.where(lane <= i, columns[i], packed)
    return jnp.transpose(packed)[0:8]


def as_columns(first, second):
    row = lax.broadcasted_iota(jnp.int32, (HEAD, TOK), 0)
    both = jnp.transpose(jnp.where(row == 0, first, second))
    return both[:, 0:1], both[:, 1:2]


def to_all(out_ref, rows):
    for i in range(N_TENSOR):
        out_ref[8 * i:8 * i + 8] = rows


def from_all(ref, row):
    return [ref[8 * i + row:8 * i + row + 1] for i in range(N_TENSOR)]


class Spread:
    def __init__(self, pivot_ref, sum_ref, square_ref):
        self.pivot, self.sum, self.square = pivot_ref, sum_ref, square_ref

    def first(self, piece):
        self.pivot[...] = jnp.broadcast_to(jnp.sum(piece, 1, keepdims=True) / HEAD, (TOK, HEAD))
        self.sum[...] = jnp.zeros_like(self.sum)
        self.square[...] = jnp.zeros_like(self.square)

    def add(self, piece):
        away = piece - self.pivot[...]
        self.sum[...] += away
        self.square[...] += away * away

    def result(self):
        away = jnp.sum(self.sum[...], 1, keepdims=True)
        square = jnp.sum(self.square[...], 1, keepdims=True)
        return away + WIDTH * self.pivot[:, 0:1], square - away * away / WIDTH


def stats_kernel(x_ref, out_ref, *scratch):
    spread = Spread(*scratch)
    spread.first(x_ref[:, 0:HEAD].astype(F32))
    for h in range(HEADS):
        spread.add(x_ref[:, h * HEAD:(h + 1) * HEAD].astype(F32))
    to_all(out_ref, as_rows(*spread.result()))


def local_stats(block):
    return pl.pallas_call(
        stats_kernel,
        in_specs=[pl.BlockSpec(memory_space=pltpu.VMEM)],
        out_specs=pl.BlockSpec(memory_space=pltpu.VMEM),
        out_shape=jax.ShapeDtypeStruct((8 * N_TENSOR, TOK), F32),
        scratch_shapes=[pltpu.VMEM((TOK, HEAD), F32)] * 3,
        cost_estimate=pl.CostEstimate(flops=8 * TOK * WIDTH, bytes_accessed=2 * TOK * WIDTH, transcendentals=0),
        compiler_params=pltpu.CompilerParams(vmem_limit_bytes=16 * 2**20),
        name="local_stats",
    )(block)


def exchange(rows):
    return lax.all_to_all(rows, "tensor", 0, 0, tiled=True)


def mean_and_scaling(stats_ref):
    sums, squares = from_all(stats_ref, SUM), from_all(stats_ref, SQUARES)
    mean = sum(sums) / D
    apart = [piece / WIDTH - mean for piece in sums]
    spread = (sum(squares) + WIDTH * sum(piece * piece for piece in apart)) / D
    return as_columns(mean, lax.rsqrt(spread + EPS))


def prepare(which, stats_ref, docs_ref, mean_ref, scaling_ref, bias_ref):
    mean, scaling = mean_and_scaling(stats_ref)
    mean_ref[...] = jnp.broadcast_to(mean, (TOK, HEAD))
    scaling_ref[...] = jnp.broadcast_to(scaling, (TOK, HEAD))
    docs = docs_ref[which:which + 1].astype(F32)
    column, _ = as_columns(docs, docs)
    t = lax.broadcasted_iota(jnp.int32, (TOK, TOK), 0)
    u = lax.broadcasted_iota(jnp.int32, (TOK, TOK), 1)
    bias_ref[...] = jnp.where((t <= u) & (column == docs), 0.0, -1e30)


def project(values, mean_ref, scaling_ref, params):
    unit = (values - mean_ref[...]) * scaling_ref[...]
    hidden = unit * params[0]
    query = (hidden * params[1]).astype(BF16)
    keyed = (hidden * params[2]).astype(BF16)
    return unit, hidden, query, keyed, hidden.astype(BF16)


def probabilities(query, keyed, bias_ref):
    scores = dot(keyed, query, ((1,), (1,))) * (SCALE * LOG2E) + bias_ref[...]
    weights = jnp.exp2(scores - jnp.max(scores, 0, keepdims=True))
    return weights * (1.0 / jnp.sum(weights, 0, keepdims=True))


def backward_kernel(
    odd_ref, stats_ref, docs_ref, params_ref, x_ref, one_ref, two_ref,
    unit_ref, act_ref, g_ref, sums_ref, section_ref,
    mean_ref, scaling_ref, bias_ref, sum_ref, cross_ref, *scratch
):
    step = pl.program_id(0)
    spread = Spread(*scratch)

    @pl.when(odd_ref[0] == 0)
    def _():
        act_ref[...] = one_ref[...]
        g_ref[...] = two_ref[...]

    @pl.when(odd_ref[0] == 1)
    def _():
        act_ref[...] = two_ref[...]
        g_ref[...] = one_ref[...]

    @pl.when(step == 0)
    def _():
        prepare(1, stats_ref, docs_ref, mean_ref, scaling_ref, bias_ref)
        sum_ref[...] = jnp.zeros_like(sum_ref)
        cross_ref[...] = jnp.zeros_like(cross_ref)
        spread.first(act_ref[:, 0:HEAD].astype(F32))

    for i in range(x_ref.shape[1] // HEAD):
        part = slice(i * HEAD, (i + 1) * HEAD)
        spread.add(act_ref[:, part].astype(F32))
        params = params_ref[:, :, part]
        unit, hidden, query, keyed, valued = project(x_ref[:, part].astype(F32), mean_ref, scaling_ref, params)
        probs = probabilities(query, keyed, bias_ref)
        g = g_ref[:, part]
        grad_vals = dot(probs.astype(BF16), g, ((1,), (0,)))
        grad_probs = dot(valued, g, ((1,), (1,)))
        centre = jnp.sum(grad_probs * probs, 0, keepdims=True)
        grad_scores = (probs * (grad_probs - centre)).astype(BF16)
        grad_query = dot(grad_scores, keyed, ((0,), (0,)))
        grad_keys = dot(grad_scores, query, ((1,), (0,)))
        grad_hidden = grad_query * (params[1] * SCALE) + grad_keys * (params[2] * SCALE) + grad_vals
        grad_unit = grad_hidden * params[0]
        unit_ref[:, part] = grad_unit
        sum_ref[...] += grad_unit
        cross_ref[...] += grad_unit * unit
        section_ref[0, :, part] = jnp.sum(grad_hidden * unit, 0, keepdims=True)
        section_ref[1, :, part] = jnp.sum(grad_query * hidden, 0, keepdims=True) * SCALE
        section_ref[2, :, part] = jnp.sum(grad_keys * hidden, 0, keepdims=True) * SCALE

    @pl.when(step == pl.num_programs(0) - 1)
    def _():
        total, squares = spread.result()
        grad = jnp.sum(sum_ref[...], 1, keepdims=True)
        cross = jnp.sum(cross_ref[...], 1, keepdims=True)
        to_all(sums_ref, as_rows(total, squares, cross, grad))


def finish_kernel(
    stats_ref, sums_ref, docs_ref, params_ref, gathered_ref, act_ref, x_ref, g_ref, unit_ref,
    new_act_ref, new_grad_ref, summed_ref,
    mean_ref, scaling_ref, bias_ref, own_ref,
):
    @pl.when(pl.program_id(0) == 0)
    def _():
        prepare(0, sums_ref, docs_ref, mean_ref, scaling_ref, bias_ref)
        mean, scaling = mean_and_scaling(stats_ref)
        mean_grad, mean_cross = as_columns(
            sum(from_all(sums_ref, GRAD)) / D, sum(from_all(sums_ref, CROSS)) / D
        )
        for i, column in enumerate((mean, scaling, mean_grad, mean_cross)):
            own_ref[i] = jnp.broadcast_to(column, (TOK, HEAD))

    for k in range(3):
        summed_ref[k] = sum(gathered_ref[r, k] for r in range(N_DP))

    for i in range(x_ref.shape[1] // HEAD):
        part = slice(i * HEAD, (i + 1) * HEAD)
        unit = (x_ref[:, part].astype(F32) - own_ref[0]) * own_ref[1]
        inner = unit_ref[:, part] - own_ref[2] - unit * own_ref[3]
        new_grad_ref[:, part] = (own_ref[1] * inner + g_ref[:, part].astype(F32)).astype(BF16)
        values = act_ref[:, part].astype(F32)
        _, _, query, keyed, valued = project(values, mean_ref, scaling_ref, params_ref[:, :, part])
        probs = probabilities(query, keyed, bias_ref).astype(BF16)
        new_act_ref[:, part] = (values + dot(probs, valued, ((0,), (0,)))).astype(BF16)


def whole(shape):
    return pl.BlockSpec(shape, lambda i: (0, 0))


def columns(rows, heads):
    return pl.BlockSpec((rows, heads * HEAD), lambda i: (0, i))


def layer(heads):
    return pl.BlockSpec((3, 1, heads * HEAD), lambda i: (0, 0, i))


def backward_layer(odd, stats, docs, params, block, one, two, heads=12):
    wide = columns(TOK, heads)
    return pl.pallas_call(
        backward_kernel,
        grid=(HEADS // heads,),
        in_specs=[pl.BlockSpec(memory_space=pltpu.SMEM), whole((64, TOK)), whole((2, TOK)), layer(heads)] + [wide] * 3,
        out_specs=[wide, wide, wide, whole((64, TOK)), layer(heads)],
        out_shape=[
            jax.ShapeDtypeStruct((TOK, WIDTH), F32),
            jax.ShapeDtypeStruct((TOK, WIDTH), BF16),
            jax.ShapeDtypeStruct((TOK, WIDTH), BF16),
            jax.ShapeDtypeStruct((64, TOK), F32),
            jax.ShapeDtypeStruct((3, 1, WIDTH), F32),
        ],
        scratch_shapes=[pltpu.VMEM((TOK, HEAD), F32)] * 2
        + [pltpu.VMEM((TOK, TOK), F32)]
        + [pltpu.VMEM((TOK, HEAD), F32)] * 5,
        cost_estimate=pl.CostEstimate(
            flops=10 * HEADS * TOK * TOK * HEAD, bytes_accessed=14 * TOK * WIDTH, transcendentals=HEADS * TOK * TOK
        ),
        compiler_params=pltpu.CompilerParams(vmem_limit_bytes=VMEM),
        name="backward_layer",
    )(odd, stats, docs, params, block, one, two)


def in_order_kernel(in_ref, out_ref):
    del in_ref, out_ref


def in_order(array):
    return pl.pallas_call(
        in_order_kernel,
        in_specs=[pl.BlockSpec(memory_space=pl.ANY)],
        out_specs=pl.BlockSpec(memory_space=pl.ANY),
        out_shape=jax.ShapeDtypeStruct(array.shape, array.dtype),
        input_output_aliases={0: 0},
        cost_estimate=pl.CostEstimate(flops=2 * 10**10, bytes_accessed=24 * WIDTH, transcendentals=0),
        name="in_order",
    )(array)


def finish_layer(stats, sums, docs, params, gathered, act, block, upstream, grad_unit, heads=12):
    wide = columns(TOK, heads)
    return pl.pallas_call(
        finish_kernel,
        grid=(HEADS // heads,),
        in_specs=[whole((64, TOK)), whole((64, TOK)), whole((2, TOK)), layer(heads)]
        + [pl.BlockSpec((N_DP, 3, 1, WIDTH), lambda i: (0, 0, 0, 0))]
        + [wide] * 4,
        out_specs=[wide, wide, pl.BlockSpec((3, 1, WIDTH), lambda i: (0, 0, 0))],
        out_shape=[jax.ShapeDtypeStruct((TOK, WIDTH), BF16)] * 2 + [jax.ShapeDtypeStruct((3, 1, WIDTH), F32)],
        scratch_shapes=[pltpu.VMEM((TOK, HEAD), F32)] * 2
        + [pltpu.VMEM((TOK, TOK), F32), pltpu.VMEM((4, TOK, HEAD), F32)],
        cost_estimate=pl.CostEstimate(
            flops=4 * HEADS * TOK * TOK * HEAD, bytes_accessed=14 * TOK * WIDTH, transcendentals=HEADS * TOK * TOK
        ),
        compiler_params=pltpu.CompilerParams(vmem_limit_bytes=VMEM),
        name="finish_layer",
    )(stats, sums, docs, params, gathered, act, block, upstream, grad_unit)


def mirror(j):
    return 15 - j


def odd_swap(j):
    return j + 1 if j % 2 else j - 1


def even_swap(j):
    return j - 1 if j % 2 else j + 1


def near(j):
    return 14 - j if j % 4 != 1 else None


def far(j):
    return 14 - j if j % 4 == 1 else None


def relay_in(j):
    return j + 2 if j % 4 == 1 else None


def relay_out(j):
    return 16 - j if j % 4 == 3 else None


def local(sent_act, sent_grad, evicted, layer_params, doc_ids):
    act, grad, stash = sent_act[0, 0], sent_grad[0, 0], evicted[0, 0]
    params, docs = jnp.transpose(layer_params, (1, 0, 2)), doc_ids[0, 0]
    place = lax.axis_index("pipe").astype(jnp.int32)
    odd = place & 1

    bwd_in = move(stash, mirror)
    swapped_odd = move(jnp.where(odd == 1, act, grad), odd_swap)
    swapped_even = move(jnp.where(odd == 1, grad, act), even_swap)

    relayed = move(act[HALF:], relay_in)
    stats = exchange(local_stats(bwd_in))
    later_act, swapped_odd, swapped_even = lax.optimization_barrier((act, swapped_odd, swapped_even))
    kept_near = move(later_act, near)
    relayed = move(relayed, relay_out)
    grad_unit, fwd_in, up_grad, sums, section_grad = backward_layer(
        odd.reshape(1), stats, docs, params, bwd_in, swapped_odd, swapped_even
    )
    sums = exchange(sums)
    gathered = lax.all_gather(in_order(section_grad), "dp")
    sums, gathered = lax.optimization_barrier((sums, gathered))
    new_act, new_grad, summed = finish_layer(
        stats, sums, docs, params, gathered, fwd_in, bwd_in, up_grad, grad_unit
    )
    last_act, new_grad = lax.optimization_barrier((act[:HALF], new_grad))
    kept_far = move(last_act, far)
    kept_input = jnp.where(place & 3 == 1, jnp.concatenate([kept_far, relayed], 0), kept_near)
    return (new_act[None, None], new_grad[None, None], kept_input[None, None], jnp.transpose(summed, (1, 0, 2)))


def solution(mesh):
    blocks = P("dp", "pipe", None, "tensor")
    weights = P("pipe", None, "tensor")
    return jax.shard_map(
        local,
        mesh=mesh,
        in_specs=(blocks, blocks, blocks, weights, P("dp", "pipe", None, None)),
        out_specs=(blocks, blocks, blocks, weights),
        check_vma=False,
    )
```

```python
import jax
import jax.numpy as jnp
from jax import lax
from jax.experimental import pallas as pl
from jax.experimental.pallas import tpu as pltpu
from jax.sharding import PartitionSpec as P

D = 12288
HEAD = 128
HALF = 128
TOK = 256
N_TENSOR = 8
N_DP = 4
WIDTH = D // N_TENSOR
HEADS = WIDTH // HEAD
SCALE = HEAD ** (-0.5)
EPS = 1e-05
LOG2E = 1.4426950408889634
SUM, SQUARES, CROSS, GRAD = 0, 1, 2, 3
F32 = jnp.float32
BF16 = jnp.bfloat16
VMEM = 56 * 2**20


def move(block, route):
    count = lax.axis_size("pipe")
    pairs = [(j, route(j) % count) for j in range(count) if route(j) is not None]
    return lax.ppermute(block, "pipe", pairs)


def dot(left, right, dims):
    return lax.dot_general(left, right, (dims, ((), ())), preferred_element_type=F32)


def as_rows(*columns):
    lane = lax.broadcasted_iota(jnp.int32, (TOK, HEAD), 1)
    packed = jnp.broadcast_to(columns[-1], (TOK, HEAD))
    for i in range(len(columns) - 2, -1, -1):
        packed = jnp.where(lane <= i, columns[i], packed)
    return jnp.transpose(packed)[0:8]


def as_columns(first, second):
    row = lax.broadcasted_iota(jnp.int32, (HEAD, TOK), 0)
    both = jnp.transpose(jnp.where(row == 0, first, second))
    return both[:, 0:1], both[:, 1:2]


def to_all(out_ref, rows):
    for i in range(N_TENSOR):
        out_ref[8 * i:8 * i + 8] = rows


def from_all(ref, row):
    return [ref[8 * i + row:8 * i + row + 1] for i in range(N_TENSOR)]


class Spread:
    def __init__(self, pivot_ref, sum_ref, square_ref):
        self.pivot, self.sum, self.square = pivot_ref, sum_ref, square_ref

    def first(self, piece):
        self.pivot[...] = jnp.broadcast_to(jnp.sum(piece, 1, keepdims=True) / HEAD, (TOK, HEAD))
        self.sum[...] = jnp.zeros_like(self.sum)
        self.square[...] = jnp.zeros_like(self.square)

    def add(self, piece):
        away = piece - self.pivot[...]
        self.sum[...] += away
        self.square[...] += away * away

    def result(self):
        away = jnp.sum(self.sum[...], 1, keepdims=True)
        square = jnp.sum(self.square[...], 1, keepdims=True)
        return away + WIDTH * self.pivot[:, 0:1], square - away * away / WIDTH


def stats_kernel(x_ref, out_ref, *scratch):
    spread = Spread(*scratch)
    spread.first(x_ref[:, 0:HEAD].astype(F32))
    for h in range(HEADS):
        spread.add(x_ref[:, h * HEAD:(h + 1) * HEAD].astype(F32))
    to_all(out_ref, as_rows(*spread.result()))


def local_stats(block):
    return pl.pallas_call(
        stats_kernel,
        in_specs=[pl.BlockSpec(memory_space=pltpu.VMEM)],
        out_specs=pl.BlockSpec(memory_space=pltpu.VMEM),
        out_shape=jax.ShapeDtypeStruct((8 * N_TENSOR, TOK), F32),
        scratch_shapes=[pltpu.VMEM((TOK, HEAD), F32)] * 3,
        cost_estimate=pl.CostEstimate(flops=8 * TOK * WIDTH, bytes_accessed=2 * TOK * WIDTH, transcendentals=0),
        compiler_params=pltpu.CompilerParams(vmem_limit_bytes=16 * 2**20),
        name="local_stats",
    )(block)


def exchange(rows):
    return lax.all_to_all(rows, "tensor", 0, 0, tiled=True)


def mean_and_scaling(stats_ref):
    sums, squares = from_all(stats_ref, SUM), from_all(stats_ref, SQUARES)
    mean = sum(sums) / D
    apart = [piece / WIDTH - mean for piece in sums]
    spread = (sum(squares) + WIDTH * sum(piece * piece for piece in apart)) / D
    return as_columns(mean, lax.rsqrt(spread + EPS))


def prepare(which, stats_ref, docs_ref, mean_ref, scaling_ref, bias_ref):
    mean, scaling = mean_and_scaling(stats_ref)
    mean_ref[...] = jnp.broadcast_to(mean, (TOK, HEAD))
    scaling_ref[...] = jnp.broadcast_to(scaling, (TOK, HEAD))
    docs = docs_ref[which:which + 1].astype(F32)
    column, _ = as_columns(docs, docs)
    t = lax.broadcasted_iota(jnp.int32, (TOK, TOK), 0)
    u = lax.broadcasted_iota(jnp.int32, (TOK, TOK), 1)
    bias_ref[...] = jnp.where((t <= u) & (column == docs), 0.0, -1e30)


def project(values, mean_ref, scaling_ref, params):
    unit = (values - mean_ref[...]) * scaling_ref[...]
    hidden = unit * params[0]
    query = (hidden * params[1]).astype(BF16)
    keyed = (hidden * params[2]).astype(BF16)
    return unit, hidden, query, keyed, hidden.astype(BF16)


def probabilities(query, keyed, bias_ref):
    scores = dot(keyed, query, ((1,), (1,))) * (SCALE * LOG2E) + bias_ref[...]
    weights = jnp.exp2(scores - jnp.max(scores, 0, keepdims=True))
    return weights * (1.0 / jnp.sum(weights, 0, keepdims=True))


def backward_kernel(
    odd_ref, stats_ref, docs_ref, params_ref, x_ref, one_ref, two_ref,
    unit_ref, act_ref, g_ref, sums_ref, section_ref,
    mean_ref, scaling_ref, bias_ref, sum_ref, cross_ref, *scratch
):
    step = pl.program_id(0)
    spread = Spread(*scratch)

    @pl.when(odd_ref[0] == 0)
    def _():
        act_ref[...] = one_ref[...]
        g_ref[...] = two_ref[...]

    @pl.when(odd_ref[0] == 1)
    def _():
        act_ref[...] = two_ref[...]
        g_ref[...] = one_ref[...]

    @pl.when(step == 0)
    def _():
        prepare(1, stats_ref, docs_ref, mean_ref, scaling_ref, bias_ref)
        sum_ref[...] = jnp.zeros_like(sum_ref)
        cross_ref[...] = jnp.zeros_like(cross_ref)
        spread.first(act_ref[:, 0:HEAD].astype(F32))

    for i in range(x_ref.shape[1] // HEAD):
        part = slice(i * HEAD, (i + 1) * HEAD)
        spread.add(act_ref[:, part].astype(F32))
        params = params_ref[:, :, part]
        unit, hidden, query, keyed, valued = project(x_ref[:, part].astype(F32), mean_ref, scaling_ref, params)
        probs = probabilities(query, keyed, bias_ref)
        g = g_ref[:, part]
        grad_vals = dot(probs.astype(BF16), g, ((1,), (0,)))
        grad_probs = dot(valued, g, ((1,), (1,)))
        centre = jnp.sum(grad_probs * probs, 0, keepdims=True)
        grad_scores = (probs * (grad_probs - centre)).astype(BF16)
        grad_query = dot(grad_scores, keyed, ((0,), (0,)))
        grad_keys = dot(grad_scores, query, ((1,), (0,)))
        grad_hidden = grad_query * (params[1] * SCALE) + grad_keys * (params[2] * SCALE) + grad_vals
        grad_unit = grad_hidden * params[0]
        unit_ref[:, part] = grad_unit
        sum_ref[...] += grad_unit
        cross_ref[...] += grad_unit * unit
        section_ref[0, :, part] = jnp.sum(grad_hidden * unit, 0, keepdims=True)
        section_ref[1, :, part] = jnp.sum(grad_query * hidden, 0, keepdims=True) * SCALE
        section_ref[2, :, part] = jnp.sum(grad_keys * hidden, 0, keepdims=True) * SCALE

    @pl.when(step == pl.num_programs(0) - 1)
    def _():
        total, squares = spread.result()
        grad = jnp.sum(sum_ref[...], 1, keepdims=True)
        cross = jnp.sum(cross_ref[...], 1, keepdims=True)
        to_all(sums_ref, as_rows(total, squares, cross, grad))


def finish_kernel(
    stats_ref, sums_ref, docs_ref, params_ref, gathered_ref, act_ref, x_ref, g_ref, unit_ref,
    new_act_ref, new_grad_ref, summed_ref,
    mean_ref, scaling_ref, bias_ref, own_ref,
):
    @pl.when(pl.program_id(0) == 0)
    def _():
        prepare(0, sums_ref, docs_ref, mean_ref, scaling_ref, bias_ref)
        mean, scaling = mean_and_scaling(stats_ref)
        mean_grad, mean_cross = as_columns(
            sum(from_all(sums_ref, GRAD)) / D, sum(from_all(sums_ref, CROSS)) / D
        )
        for i, column in enumerate((mean, scaling, mean_grad, mean_cross)):
            own_ref[i] = jnp.broadcast_to(column, (TOK, HEAD))

    for k in range(3):
        summed_ref[k] = sum(gathered_ref[r, k] for r in range(N_DP))

    for i in range(x_ref.shape[1] // HEAD):
        part = slice(i * HEAD, (i + 1) * HEAD)
        unit = (x_ref[:, part].astype(F32) - own_ref[0]) * own_ref[1]
        inner = unit_ref[:, part] - own_ref[2] - unit * own_ref[3]
        new_grad_ref[:, part] = (own_ref[1] * inner + g_ref[:, part].astype(F32)).astype(BF16)
        values = act_ref[:, part].astype(F32)
        _, _, query, keyed, valued = project(values, mean_ref, scaling_ref, params_ref[:, :, part])
        probs = probabilities(query, keyed, bias_ref).astype(BF16)
        new_act_ref[:, part] = (values + dot(probs, valued, ((0,), (0,)))).astype(BF16)


def whole(shape):
    return pl.BlockSpec(shape, lambda i: (0, 0))


def columns(rows, heads):
    return pl.BlockSpec((rows, heads * HEAD), lambda i: (0, i))


def layer(heads):
    return pl.BlockSpec((3, 1, heads * HEAD), lambda i: (0, 0, i))


def backward_layer(odd, stats, docs, params, block, one, two, heads=12):
    wide = columns(TOK, heads)
    return pl.pallas_call(
        backward_kernel,
        grid=(HEADS // heads,),
        in_specs=[pl.BlockSpec(memory_space=pltpu.SMEM), whole((64, TOK)), whole((2, TOK)), layer(heads)] + [wide] * 3,
        out_specs=[wide, wide, wide, whole((64, TOK)), layer(heads)],
        out_shape=[
            jax.ShapeDtypeStruct((TOK, WIDTH), F32),
            jax.ShapeDtypeStruct((TOK, WIDTH), BF16),
            jax.ShapeDtypeStruct((TOK, WIDTH), BF16),
            jax.ShapeDtypeStruct((64, TOK), F32),
            jax.ShapeDtypeStruct((3, 1, WIDTH), F32),
        ],
        scratch_shapes=[pltpu.VMEM((TOK, HEAD), F32)] * 2
        + [pltpu.VMEM((TOK, TOK), F32)]
        + [pltpu.VMEM((TOK, HEAD), F32)] * 5,
        cost_estimate=pl.CostEstimate(
            flops=10 * HEADS * TOK * TOK * HEAD, bytes_accessed=14 * TOK * WIDTH, transcendentals=HEADS * TOK * TOK
        ),
        compiler_params=pltpu.CompilerParams(vmem_limit_bytes=VMEM),
        name="backward_layer",
    )(odd, stats, docs, params, block, one, two)


def in_order_kernel(in_ref, out_ref):
    del in_ref, out_ref


def in_order(array):
    return pl.pallas_call(
        in_order_kernel,
        in_specs=[pl.BlockSpec(memory_space=pl.ANY)],
        out_specs=pl.BlockSpec(memory_space=pl.ANY),
        out_shape=jax.ShapeDtypeStruct(array.shape, array.dtype),
        input_output_aliases={0: 0},
        cost_estimate=pl.CostEstimate(flops=2 * 10**10, bytes_accessed=24 * WIDTH, transcendentals=0),
        name="in_order",
    )(array)


def finish_layer(stats, sums, docs, params, gathered, act, block, upstream, grad_unit, heads=12):
    wide = columns(TOK, heads)
    return pl.pallas_call(
        finish_kernel,
        grid=(HEADS // heads,),
        in_specs=[whole((64, TOK)), whole((64, TOK)), whole((2, TOK)), layer(heads)]
        + [pl.BlockSpec((N_DP, 3, 1, WIDTH), lambda i: (0, 0, 0, 0))]
        + [wide] * 4,
        out_specs=[wide, wide, pl.BlockSpec((3, 1, WIDTH), lambda i: (0, 0, 0))],
        out_shape=[jax.ShapeDtypeStruct((TOK, WIDTH), BF16)] * 2 + [jax.ShapeDtypeStruct((3, 1, WIDTH), F32)],
        scratch_shapes=[pltpu.VMEM((TOK, HEAD), F32)] * 2
        + [pltpu.VMEM((TOK, TOK), F32), pltpu.VMEM((4, TOK, HEAD), F32)],
        cost_estimate=pl.CostEstimate(
            flops=4 * HEADS * TOK * TOK * HEAD, bytes_accessed=14 * TOK * WIDTH, transcendentals=HEADS * TOK * TOK
        ),
        compiler_params=pltpu.CompilerParams(vmem_limit_bytes=107 * 2**19),
        name="finish_layer",
    )(stats, sums, docs, params, gathered, act, block, upstream, grad_unit)


def mirror(j):
    return 15 - j


def odd_swap(j):
    return j + 1 if j % 2 else j - 1


def even_swap(j):
    return j - 1 if j % 2 else j + 1


def near(j):
    return 14 - j if j % 4 != 1 else None


def far(j):
    return 14 - j if j % 4 == 1 else None


def relay_in(j):
    return j + 2 if j % 4 == 1 else None


def relay_out(j):
    return 16 - j if j % 4 == 3 else None


def local(sent_act, sent_grad, evicted, layer_params, doc_ids):
    act, grad, stash = sent_act[0, 0], sent_grad[0, 0], evicted[0, 0]
    params, docs = jnp.transpose(layer_params, (1, 0, 2)), doc_ids[0, 0]
    place = lax.axis_index("pipe").astype(jnp.int32)
    odd = place & 1

    bwd_in = move(stash, mirror)
    swapped_odd = move(jnp.where(odd == 1, act, grad), odd_swap)
    swapped_even = move(jnp.where(odd == 1, grad, act), even_swap)

    relayed = move(act[HALF:], relay_in)
    stats = exchange(local_stats(bwd_in))
    later_act, swapped_odd, swapped_even = lax.optimization_barrier((act, swapped_odd, swapped_even))
    kept_near = move(later_act, near)
    relayed = move(relayed, relay_out)
    grad_unit, fwd_in, up_grad, sums, section_grad = backward_layer(
        odd.reshape(1), stats, docs, params, bwd_in, swapped_odd, swapped_even
    )
    sums = exchange(sums)
    gathered = lax.all_gather(in_order(section_grad), "dp")
    sums, gathered = lax.optimization_barrier((sums, gathered))
    new_act, new_grad, summed = finish_layer(
        stats, sums, docs, params, gathered, fwd_in, bwd_in, up_grad, grad_unit
    )
    last_act, new_grad = lax.optimization_barrier((act[:HALF], new_grad))
    kept_far = move(last_act, far)
    kept_input = jnp.where(place & 3 == 1, jnp.concatenate([kept_far, relayed], 0), kept_near)
    return (new_act[None, None], new_grad[None, None], kept_input[None, None], jnp.transpose(summed, (1, 0, 2)))


def solution(mesh):
    blocks = P("dp", "pipe", None, "tensor")
    weights = P("pipe", None, "tensor")
    return jax.shard_map(
        local,
        mesh=mesh,
        in_specs=(blocks, blocks, blocks, weights, P("dp", "pipe", None, None)),
        out_specs=(blocks, blocks, blocks, weights),
        check_vma=False,
    )
```
